32 devices in a mesh: expert: 8 (over z, x), dp: 4 (over y, core).
Axes of the slice: x: 2, y: 2, z: 4, core: 2. Of those that a mesh axis runs over, the one named last changes fastest.
Arguments:
- inputs: bfloat16 [4096, 2048], P(('expert', 'dp')), may hold values from -6 to 6
- layer_out: bfloat16 [4096, 2048], P(('expert', 'dp')), may hold values from -6 to 6
- teacher: bfloat16 [4096, 2048], P(('expert', 'dp')), may hold values from -6 to 6
- alignment: bfloat16 [4096, 128], P(('expert', 'dp')), may hold values from 0 to 1.5
- routes: int32 [4096, 2], P(('expert', 'dp')), may hold values from 0 to 7, all different within a row; in each aligned block of 128 rows (0 to 127, 128 to 255, ...) at most 40 rows name the same one
- route_weights: bfloat16 [4096, 2], P(('expert', 'dp')), may hold values from 0.19921875 to 1
- partner: int32 [32], P(('expert', 'dp')), may hold values from 0 to 3
- w_gate: bfloat16 [8, 2048, 1408], P('expert', None, 'dp'), may hold values from -0.125 to 0.125
- w_up: bfloat16 [8, 2048, 1408], P('expert', None, 'dp'), may hold values from -0.125 to 0.125
- w_down: bfloat16 [8, 1408, 2048], P('expert', 'dp'), may hold values from -0.15625 to 0.15625
Outputs:
- grad_inputs: bfloat16 [4096, 2048], P(('expert', 'dp'))
- grad_gate: bfloat16 [8, 2048, 1408], P('expert', None, 'dp')
- grad_up: bfloat16 [8, 2048, 1408], P('expert', None, 'dp')
- grad_down: bfloat16 [8, 1408, 2048], P('expert', 'dp')
The draws below stay inside these ranges and needn't reach their ends.
Inputs may be any that keep to these rules, and one draw needn't show every extreme that they name: `routes`: each row names 2 different experts. The rows of one device name any one expert at most 40 times, and some device names some expert exactly 40 times.
All inputs are finite; a program needn't handle non-finite values.
Results may differ from the reference program's by a relative error of at most 0.019.
Values may be sent and summed in bfloat16 or wider, within the bound.
No kernel may reach another device: no remote copies, remote signals or barrier semaphores. Data moves between devices by JAX's collectives and lax.ppermute only.
A program may use at most 128 MiB of HBM per device.

```python
import math
import jax
import jax.numpy as jnp
import numpy as np
from jax import lax

D = 2048
FF = 1408
TOP = 2
TOK_DEV = 128
EXPERTS = 8
CAP = 40
QUARTER = 352
TOKENS = 4096
N_DP = 4
DEVICES = 32


def draw_alignment(key, part):
    row_pos = (jnp.arange(TOKENS, dtype=jnp.int32) % TOK_DEV).astype(jnp.float32)
    col_pos = jnp.arange(TOK_DEV, dtype=jnp.int32).astype(jnp.float32)
    distance = jnp.abs(row_pos[:, None] - col_pos[None, :])
    factor = jax.random.uniform(key, (TOKENS, TOK_DEV), jnp.float32, 0.2, 1.0)
    values = factor * jnp.exp(-distance / 3.0)
    return values.astype(jnp.bfloat16)


def touch_ends(drawn, rng, least, high):
    extent = drawn.shape
    index_at = [jax.random.randint(jax.random.fold_in(rng, axis), (), 0, extent[axis]) for axis in range(len(extent))]
    drawn = drawn.at[tuple(index_at)].set(least)
    longest = extent.index(max(extent))
    index_at[longest] = (index_at[longest] + 1) % extent[longest]
    return drawn.at[tuple(index_at)].set(high)


def levels(key, dims, pieces, smallest, top_value):
    factor_of, own = 1.0, jax.random.fold_in(key, 6)
    for axis_at, shards_of in pieces:
        heights = jnp.exp(jax.random.uniform(jax.random.fold_in(own, axis_at), (shards_of,), jnp.float32, smallest / len(pieces), top_value / len(pieces)))
        factor_of = factor_of * jnp.repeat(heights, dims[axis_at] // shards_of).reshape([-1 if axis == axis_at else 1 for axis in range(len(dims))])
    return factor_of


def shared_out(stream_key, own, number, rows, count, top, reach, slope):
    sequence = jax.random.permutation(stream_key, count)
    heavy_load, ordinary = shares(count, rows * top, reach, slope, True), shares(count, rows * top, reach, slope, False)
    places = jnp.arange(count)

    def named(lengths, offset_by):
        used = int((lengths > 0).sum())
        fixed = max(1, used // 4)
        moved = fixed + (places - fixed + offset_by * (used - fixed)) % max(1, count - fixed)
        return jnp.zeros((count,), jnp.int32).at[sequence[jnp.where(places < fixed, places, moved)]].set(jnp.asarray(lengths, jnp.int32))

    lengths = jnp.where(number % 4 == 0, named(heavy_load, number // 4), named(ordinary, number - number // 4 - 1))
    mixed = jax.random.permutation(jax.random.fold_in(own, 3), count)
    giver, receiver = mixed[0:count // 2 * 2:2], mixed[1:count // 2 * 2:2]
    room = jnp.minimum(lengths[giver] - 1, reach - lengths[receiver]) // 2
    room = jnp.where((giver == sequence[0]) | (receiver == sequence[0]) | (lengths[receiver] == 0), 0, jnp.maximum(room, 0))
    moved = jax.random.randint(jax.random.fold_in(own, 4), (count // 2,), 0, 1 << 20) % (room + 1)
    lengths = lengths.at[giver].add(-moved).at[receiver].add(moved)
    items = jnp.searchsorted(jnp.cumsum(lengths), jnp.arange(rows * top), side="right").astype(jnp.int32)
    grid = items.reshape(top, rows).T
    grid = grid[jax.random.permutation(jax.random.fold_in(own, 1), rows)]
    offset_by = jax.random.randint(jax.random.fold_in(own, 2), (rows, 1), 0, top)
    return jnp.take_along_axis(grid, (jnp.arange(top)[None, :] + offset_by) % top, axis=1)


def shares(amount, total, most, skew, full):
    portions = [(1 << 20) // math.isqrt(rank ** skew) + 1 for rank in range(1, amount + 1)]
    largest = most if full else min(most, max(-(-total // amount), total * portions[0] // sum(portions)))
    least = 1 if total - largest >= amount - 1 else 0
    counts, rest = [largest] + [least] * (amount - 1), total - largest - least * (amount - 1)
    while rest > 0:
        movable = [i for i in range(1, amount) if counts[i] < largest] or [i for i in range(1, amount) if counts[i] < most]
        whole, remaining = sum([portions[i] for i in movable]), rest
        for i in movable:
            extra = min(most - counts[i], max(1, remaining * portions[i] // whole), rest)
            counts[i] = counts[i] + extra
            rest = rest - extra
    return np.array(counts)


def normal_values(own_key, dims, scale, limit, shards=(), kind=jnp.bfloat16):
    drawn = scale * jax.random.normal(own_key, dims, jnp.float32)
    if shards:
        drawn = drawn * levels(own_key, dims, shards, -0.22, 0.18)
    return jnp.clip(drawn, -limit, limit).astype(kind)


def setup_inputs(seed: int = 0) -> dict:
    splits = jax.random.split(jax.random.key(seed), 11)
    inputs = normal_values(splits[0], (TOKENS, D), 1.0, 6.0, ((0, 32),))
    layer_out = normal_values(splits[1], (TOKENS, D), 1.0, 6.0, ((0, 32),))
    teacher = normal_values(splits[2], (TOKENS, D), 1.0, 6.0, ((0, 32),))
    alignment = draw_alignment(jax.random.fold_in(splits[10], 71), 0)
    routes_keys = jax.random.split(jax.random.fold_in(splits[4], 1), TOKENS // TOK_DEV)
    routes_turns = jax.random.permutation(jax.random.fold_in(splits[4], 3), TOKENS // TOK_DEV)
    routes = jax.vmap(lambda own, number: shared_out(jax.random.fold_in(splits[4], 2), own, number, TOK_DEV, EXPERTS, TOP, CAP, 2))(routes_keys, routes_turns).reshape((TOKENS, TOP))
    route_weights = jnp.clip(0.19921875 + 0.80078125 * jax.random.uniform(splits[5], (TOKENS, TOP), jnp.float32) ** levels(splits[5], (TOKENS, TOP), ((0, 32),), -0.2, 0.2), 0.19921875, 1.0).astype(jnp.bfloat16)
    partner = touch_ends(jax.random.randint(splits[6], (DEVICES,), 0, N_DP), jax.random.fold_in(splits[6], 1), 0, N_DP - 1).astype(jnp.int32)
    w_gate = normal_values(splits[7], (EXPERTS, D, FF), D ** -0.5, 0.125, ((0, 8), (2, 4)))
    w_up = normal_values(splits[8], (EXPERTS, D, FF), D ** -0.5, 0.125, ((0, 8), (2, 4)))
    w_down = normal_values(splits[9], (EXPERTS, FF, D), FF ** -0.5, 0.15625, ((0, 8), (1, 4)))
    return {"inputs": inputs, "layer_out": layer_out, "teacher": teacher, "alignment": alignment, "routes": routes, "route_weights": route_weights, "partner": partner, "w_gate": w_gate, "w_up": w_up, "w_down": w_down}


def reference(inputs, layer_out, teacher, alignment, routes, route_weights, partner, w_gate, w_up, w_down):
    input_blocks = inputs.reshape(DEVICES, TOK_DEV, D)
    out_blocks = layer_out.reshape(DEVICES, TOK_DEV, D)
    teacher_blocks = teacher.reshape(DEVICES, TOK_DEV, D)
    align_blocks = alignment.reshape(DEVICES, TOK_DEV, TOK_DEV)
    source = ((jnp.arange(DEVICES, dtype=jnp.int32) // N_DP) * N_DP + partner.astype(jnp.int32)).astype(jnp.int32)
    partner_teacher = teacher_blocks[source]

    def block_cotangent(args):
        align_one, teach_one, out_one = args
        aligned = jnp.dot(align_one, teach_one, preferred_element_type=jnp.float32)
        return (out_one.astype(jnp.float32) - aligned).astype(jnp.bfloat16)

    cotangent = lax.map(block_cotangent, (align_blocks, partner_teacher, out_blocks))
    flat_routes = routes.reshape(DEVICES, TOK_DEV * TOP).astype(jnp.int32)
    one_hot = (flat_routes[:, :, None] == jnp.arange(EXPERTS, dtype=jnp.int32)[None, None, :]).astype(jnp.int32)
    earlier = jnp.cumsum(one_hot, axis=1) - one_hot
    slot_index = jnp.sum(earlier * one_hot, axis=2).astype(jnp.int32)
    weights_float = route_weights.reshape(DEVICES, TOK_DEV, TOP, 1).astype(jnp.float32)
    out_grad = (weights_float * cotangent[:, :, None, :].astype(jnp.float32)).astype(jnp.bfloat16)
    out_grad = out_grad.reshape(DEVICES, TOK_DEV * TOP, D)
    input_rows = jnp.repeat(input_blocks, TOP, axis=1)
    device_ids = jnp.broadcast_to(jnp.arange(DEVICES, dtype=jnp.int32)[:, None], flat_routes.shape)
    zeros_buffer = jnp.zeros((EXPERTS, DEVICES, CAP, D), jnp.bfloat16)
    input_buffer = zeros_buffer.at[flat_routes, device_ids, slot_index].set(input_rows)
    grad_buffer = zeros_buffer.at[flat_routes, device_ids, slot_index].set(out_grad)
    highest = lax.Precision.HIGHEST

    def expert(args):
        rows_in, rows_grad, gate_weight, up_weight, down_weight = args
        input_mat = rows_in.reshape(-1, D).astype(jnp.float32)
        grad_mat = rows_grad.reshape(-1, D).astype(jnp.float32)
        gate_float = gate_weight.astype(jnp.float32)
        up_float = up_weight.astype(jnp.float32)
        down_float = down_weight.astype(jnp.float32)
        gate_term = jnp.dot(input_mat, gate_float, precision=highest)
        up_term = jnp.dot(input_mat, up_float, precision=highest)
        sigmoid_gate = jax.nn.sigmoid(gate_term)
        activated = gate_term * sigmoid_gate
        hidden = lax.optimization_barrier((activated * up_term).astype(jnp.bfloat16)).astype(jnp.float32)
        d_hidden = jnp.dot(grad_mat, down_float.T, precision=highest)
        d_gate = (d_hidden * up_term * (sigmoid_gate + activated * (1.0 - sigmoid_gate))).astype(jnp.bfloat16)
        d_up = (d_hidden * activated).astype(jnp.bfloat16)
        d_gate = lax.optimization_barrier(d_gate).astype(jnp.float32)
        d_up = lax.optimization_barrier(d_up).astype(jnp.float32)
        grad_down = jnp.dot(hidden.T, grad_mat, precision=highest).astype(jnp.bfloat16)
        grad_gate = jnp.dot(input_mat.T, d_gate, precision=highest).astype(jnp.bfloat16)
        grad_up = jnp.dot(input_mat.T, d_up, precision=highest).astype(jnp.bfloat16)
        row_total = jnp.zeros(input_mat.shape, jnp.float32)
        for quarter_index in range(N_DP):
            quarter_cols = slice(quarter_index * QUARTER, (quarter_index + 1) * QUARTER)
            partial_sum = jnp.dot(d_gate[:, quarter_cols], gate_float[:, quarter_cols].T, precision=highest)
            partial_sum = partial_sum + jnp.dot(d_up[:, quarter_cols], up_float[:, quarter_cols].T, precision=highest)
            rounded = lax.optimization_barrier(partial_sum.astype(jnp.bfloat16))
            row_total = row_total + rounded.astype(jnp.float32)
        row_grads = row_total.astype(jnp.bfloat16).reshape(DEVICES, CAP, D)
        return row_grads, grad_gate, grad_up, grad_down

    row_grads, grad_gate, grad_up, grad_down = lax.map(expert, (input_buffer, grad_buffer, w_gate, w_up, w_down))
    picked = row_grads[flat_routes, device_ids, slot_index].astype(jnp.float32)
    grad_inputs = jnp.sum(picked.reshape(DEVICES, TOK_DEV, TOP, D), axis=2).astype(jnp.bfloat16)
    return grad_inputs.reshape(TOKENS, D), grad_gate, grad_up, grad_down
```

```python
import jax
import jax.numpy as jnp
import numpy as np
from jax import lax
from jax.sharding import PartitionSpec as P

F32, BF16 = jnp.float32, jnp.bfloat16


def flip(block, axis, shift):
    if shift == 0:
        return block
    return lax.ppermute(block, axis, [(i, i ^ shift) for i in range(lax.axis_size(axis))])


def by_columns(left, right):
    return lax.dot_general(left, right, (((1,), (1,)), ((), ())), preferred_element_type=F32)


def by_rows(left, right):
    return lax.dot_general(left, right, (((0,), (0,)), ((), ())), preferred_element_type=F32)


def slot_matrices(routes, route_weights, experts, capacity):
    named = routes.T[None] == experts[:, None, None]
    weight = jnp.sum(jnp.where(named, route_weights.T[None].astype(F32), 0.0), axis=1)
    member = jnp.any(named, axis=1)
    tokens = routes.shape[0]
    before = jnp.arange(tokens)[:, None] < jnp.arange(tokens)[None, :]
    earlier = jnp.dot(member.astype(BF16), before.astype(BF16), preferred_element_type=F32)
    slots = jnp.arange(capacity, dtype=F32)[None, :, None]
    filled = member[:, None, :] & (earlier[:, None, :] == slots)
    return filled.astype(BF16), jnp.where(filled, weight[:, None, :], 0.0).astype(BF16)


def exchange_groups(expert_count):
    if expert_count == 8:
        return [(0, 1, 2, 3), (4, 5), (6, 7)]
    return [tuple(range(expert_count))]


def to_experts(blocks, groups, capacity):
    if len(groups) == 1:
        rows = blocks[0]
        got = lax.all_to_all(
            rows.reshape(-1, capacity, rows.shape[-1]), "expert", split_axis=0, concat_axis=0, tiled=True
        )
        return [got.reshape(rows.shape)]
    return [
        jnp.concatenate(
            [flip(block[n * capacity : (n + 1) * capacity], "expert", k) for n, k in enumerate(group)], axis=0
        )
        for block, group in zip(blocks, groups)
    ]


def per_device(
    inputs, layer_out, teacher, alignment, routes, route_weights, partner, w_gate, w_up, w_down
):
    tok_rows, features = inputs.shape
    route_count = routes.shape[1]
    expert_count = lax.axis_size("expert")
    capacity = max(2, (5 * tok_rows * route_count + 4 * expert_count - 1) // (4 * expert_count))
    me = lax.axis_index("expert")
    groups = exchange_groups(expert_count)

    def joined(weight, axis):
        return jnp.concatenate([weight, flip(weight, "dp", 1)], axis=axis)

    gate_weight = joined(w_gate[0], 1)
    up_weight = joined(w_up[0], 1)
    down_weight = joined(w_down[0], 0)
    quarter = w_gate.shape[2]

    order = np.array([k for group in groups for k in group], dtype=np.int32)
    experts = jnp.asarray(order) if len(groups) == 1 else jnp.asarray(order) ^ me
    filled, weighted = slot_matrices(routes, route_weights, experts, capacity)
    edges = np.cumsum([0] + [len(group) for group in groups])
    filled = [filled[a:b].reshape(-1, tok_rows) for a, b in zip(edges[:-1], edges[1:])]
    weighted = [weighted[a:b].reshape(-1, tok_rows) for a, b in zip(edges[:-1], edges[1:])]

    across = flip(teacher, "dp", 2)
    beside, beside_across = flip(teacher, "dp", 1), flip(across, "dp", 1)
    apart = partner[0] ^ lax.axis_index("dp")
    partner_teacher = jnp.where(
        apart < 2,
        jnp.where(apart == 0, teacher, beside),
        jnp.where(apart == 2, across, beside_across),
    )
    aligned = jnp.dot(alignment, partner_teacher, preferred_element_type=F32)
    cotangent = (layer_out.astype(F32) - aligned).astype(BF16)

    sent_inputs = [jnp.dot(m, inputs, preferred_element_type=F32).astype(BF16) for m in filled]
    sent_grads = [jnp.dot(m, cotangent, preferred_element_type=F32).astype(BF16) for m in weighted]
    got_inputs = to_experts(sent_inputs, groups, capacity)
    got_grads = to_experts(sent_grads, groups, capacity)
    expert_inputs = [jnp.concatenate([rows, flip(rows, "dp", 2)], axis=0) for rows in got_inputs]
    expert_grads = [jnp.concatenate([rows, flip(rows, "dp", 2)], axis=0) for rows in got_grads]

    hidden, d_gate, d_up, returned = [], [], [], []
    for rows, grads in zip(expert_inputs, expert_grads):
        gate_term = jnp.dot(rows, gate_weight, preferred_element_type=F32)
        up_term = jnp.dot(rows, up_weight, preferred_element_type=F32)
        sigmoid_gate = jax.nn.sigmoid(gate_term)
        activated = gate_term * sigmoid_gate
        hidden.append((activated * up_term).astype(BF16))
        d_hidden = by_columns(grads, down_weight)
        one_gate = (d_hidden * up_term * (sigmoid_gate + activated * (1.0 - sigmoid_gate))).astype(BF16)
        one_up = (d_hidden * activated).astype(BF16)
        d_gate.append(one_gate)
        d_up.append(one_up)
        row_sums = by_columns(one_gate, gate_weight) + by_columns(one_up, up_weight)
        half = rows.shape[0] // 2
        other = flip(row_sums[half:].astype(BF16), "dp", 2)
        returned.append((row_sums[:half] + other.astype(F32)).astype(BF16))
    back = to_experts(returned, groups, capacity)
    grad_inputs = sum(by_rows(m, rows) for m, rows in zip(filled, back)).astype(BF16)

    inputs_all = jnp.concatenate(expert_inputs, axis=0)
    grads_all = jnp.concatenate(expert_grads, axis=0)
    hidden, d_gate, d_up = (jnp.concatenate(parts, axis=0) for parts in (hidden, d_gate, d_up))

    def summed(own, other):
        return (own + flip(other.astype(BF16), "dp", 1).astype(F32)).astype(BF16)[None]

    grad_gate = summed(by_rows(inputs_all, d_gate[:, :quarter]), by_rows(inputs_all, d_gate[:, quarter:]))
    grad_up = summed(by_rows(inputs_all, d_up[:, :quarter]), by_rows(inputs_all, d_up[:, quarter:]))
    grad_down = summed(by_rows(hidden[:, :quarter], grads_all), by_rows(hidden[:, quarter:], grads_all))
    return grad_inputs, grad_gate, grad_up, grad_down


def solution(mesh):
    tokens = P(("expert", "dp"), None)
    columns, rows = P("expert", None, "dp"), P("expert", "dp", None)
    return jax.shard_map(
        per_device,
        mesh=mesh,
        in_specs=(tokens,) * 6 + (P(("expert", "dp")), columns, columns, rows),
        out_specs=(tokens, columns, columns, rows),
        check_vma=False,
    )
```

```python
import jax
import jax.numpy as jnp
import numpy as np
from jax import lax
from jax.sharding import PartitionSpec as P

F32, BF16 = jnp.float32, jnp.bfloat16


def flip(block, axis, shift, name="rows"):
    with jax.named_scope(name):
        return lax.ppermute(block, axis, [(i, i ^ shift) for i in range(lax.axis_size(axis))])


def by_columns(left, right):
    return lax.dot_general(left, right, (((1,), (1,)), ((), ())), preferred_element_type=F32)


def by_rows(left, right):
    return lax.dot_general(left, right, (((0,), (0,)), ((), ())), preferred_element_type=F32)


def slot_matrices(routes, route_weights, experts, capacity):
    named = routes.T[None] == experts[:, None, None]
    weight = jnp.sum(jnp.where(named, route_weights.T[None].astype(F32), 0.0), axis=1)
    member = jnp.any(named, axis=1)
    tokens = routes.shape[0]
    before = jnp.arange(tokens)[:, None] < jnp.arange(tokens)[None, :]
    earlier = jnp.dot(member.astype(BF16), before.astype(BF16), preferred_element_type=F32)
    slots = jnp.arange(capacity, dtype=F32)[None, :, None]
    filled = member[:, None, :] & (earlier[:, None, :] == slots)
    return filled.astype(BF16), jnp.where(filled, weight[:, None, :], 0.0).astype(BF16)


def after(block, *earlier):
    return lax.optimization_barrier((block, earlier))[0]


def partner_rows(teacher, across, beside, partner):
    tok_rows = teacher.shape[0]
    apart = partner[0] ^ lax.axis_index("dp")
    return jnp.where(
        apart < 2,
        jnp.where(apart == 0, teacher, beside[:tok_rows]),
        jnp.where(apart == 2, across, beside[tok_rows:]),
    )


def spread(matrices, rows):
    return jnp.dot(matrices, rows, preferred_element_type=F32).astype(BF16)


def grad_halves(inputs, grads, kept):
    inputs, grads = jnp.concatenate(inputs, axis=0), jnp.concatenate(grads, axis=0)
    hidden, d_gate, d_up = (jnp.concatenate(parts, axis=0) for parts in zip(*kept))
    quarter = hidden.shape[1] // 2
    own, other = slice(0, quarter), slice(quarter, None)
    side = by_rows(jnp.concatenate([d_gate[:, other], d_up[:, other]], axis=1), inputs).astype(BF16)
    down = by_rows(hidden[:, other], grads).astype(BF16)
    return (
        ((d_gate[:, own], inputs), (d_up[:, own], inputs), (hidden[:, own], grads)),
        jnp.concatenate([side, down], axis=0),
    )


def grad_totals(own, other):
    parts = jnp.split(other, 3, axis=0)
    gate, up, down = ((by_rows(*mine) + part.astype(F32)).astype(BF16) for mine, part in zip(own, parts))
    return gate.T[None], up.T[None], down[None]


def per_device(
    inputs, layer_out, teacher, alignment, routes, route_weights, partner, w_gate, w_up, w_down
):
    tok_rows, features = inputs.shape
    route_count = routes.shape[1]
    expert_count = lax.axis_size("expert")
    capacity = max(2, (5 * tok_rows * route_count + 4 * expert_count - 1) // (4 * expert_count))
    me = lax.axis_index("expert")
    quarter = w_gate.shape[2]
    small = expert_count == 8

    across = flip(teacher, "dp", 2, "teacher_across")

    experts = jnp.arange(expert_count, dtype=jnp.int32)
    filled, weighted = slot_matrices(routes, route_weights, experts ^ me if small else experts, capacity)

    def pick(matrices, shifts):
        return jnp.concatenate([matrices[k] for k in shifts], axis=0)

    def expert_rows(rows, half, grads):
        gate_term = jnp.dot(rows, gate_weight, preferred_element_type=F32)
        up_term = jnp.dot(rows, up_weight, preferred_element_type=F32)
        sigmoid_gate = jax.nn.sigmoid(gate_term)
        activated = gate_term * sigmoid_gate
        hidden = (activated * up_term).astype(BF16)
        d_hidden = by_columns(grads, down_weight)
        d_gate = (d_hidden * up_term * (sigmoid_gate + activated * (1.0 - sigmoid_gate))).astype(BF16)
        d_up = (d_hidden * activated).astype(BF16)
        sums = by_columns(d_gate, gate_weight) + by_columns(d_up, up_weight)
        return (hidden, d_gate, d_up), sums[:half], sums[half:].astype(BF16)

    def both(rows, other):
        return jnp.concatenate([rows, other], axis=0)

    def total(own, other):
        return (own + other.astype(F32)).astype(BF16)

    def join_weights(gate_other, up_other, down_other):
        return (
            jnp.concatenate([w_gate[0], gate_other], axis=1),
            jnp.concatenate([w_up[0], up_other], axis=1),
            jnp.concatenate([w_down[0], down_other], axis=0),
        )

    if small:
        c = capacity

        x_side = flip(spread(pick(filled, (1, 3, 7)), inputs), "expert", 1, "inputs_side")
        x_far = [flip(spread(filled[k], inputs), "expert", k, f"inputs_far_{k}") for k in (4, 5)]
        beside = flip(jnp.concatenate([teacher, across], axis=0), "dp", 1, "teacher_beside")

        x_own, near2, near6 = [spread(after(filled[k], across), inputs) for k in (0, 2, 6)]
        xa = jnp.concatenate([x_own, x_side[:c]] + x_far, axis=0)
        partner_teacher = partner_rows(teacher, across, beside, partner)
        aligned = jnp.dot(alignment, partner_teacher, preferred_element_type=F32)
        cotangent = (layer_out.astype(F32) - aligned).astype(BF16)
        g_send = spread(pick(weighted, (1, 3, 5, 7)), cotangent)
        g_side = flip(g_send, "expert", 1, "grads_side")
        ya = flip(after(xa, g_send), "dp", 2, "inputs_a")
        x_z3 = flip(after(jnp.concatenate([near6, x_side[2 * c :]], axis=0), x_far, g_send), "expert", 6, "inputs_z3")
        x_z1 = flip(after(jnp.concatenate([near2, x_side[c : 2 * c]], axis=0), x_far, g_send), "expert", 2, "inputs_z1")
        g_own, gear2, gear4, gear6 = [spread(weighted[k], cotangent) for k in (0, 2, 4, 6)]
        gate_other = flip(after(w_gate[0], cotangent), "dp", 1, "gate_weight")
        xb = jnp.concatenate([x_z1, x_z3], axis=0)

        yb = flip(after(xb, ya, g_side), "dp", 2, "inputs_b")
        g_z2 = flip(after(jnp.concatenate([gear4, g_side[2 * c : 3 * c]], axis=0), x_z3, x_z1), "expert", 4, "grads_z2")
        g_z1 = flip(after(jnp.concatenate([gear2, g_side[c : 2 * c]], axis=0), x_z3, x_z1), "expert", 2, "grads_z1")
        up_other = flip(after(w_up[0], gate_other, x_z3), "dp", 1, "up_weight")

        ga = jnp.concatenate([g_own, g_side[:c], g_z2], axis=0)
        ha = flip(after(ga, yb), "dp", 2, "grads_a")
        g_z3 = flip(after(jnp.concatenate([gear6, g_side[3 * c :]], axis=0), g_z2), "expert", 6, "grads_z3")
        down_other = flip(after(w_down[0], up_other, yb), "dp", 1, "down_weight")
        gate_weight, up_weight, down_weight = join_weights(gate_other, up_other, down_other)

        gb = jnp.concatenate([g_z1, g_z3], axis=0)
        hb = flip(after(gb, ha, down_other), "dp", 2, "grads_b")
        expert_inputs = [both(xa, ya), both(xb, yb)]
        expert_grads = [both(ga, ha), both(gb, hb)]
        kept, own_sums, other_sums = zip(
            *[expert_rows(r, r.shape[0] // 2, g) for r, g in zip(expert_inputs, expert_grads)]
        )

        sa = flip(after(other_sums[0], hb), "dp", 2, "sums_a")
        ra = total(own_sums[0], sa)

        step = (sa, other_sums[1])
        sb = flip(after(other_sums[1], step), "dp", 2, "sums_b")
        back = {0: ra[:c]}
        for n, k in enumerate((1, 4, 5), 1):
            back[k] = flip(after(ra[n * c : (n + 1) * c], step), "expert", k, f"returned_{k}")
        rb = total(own_sums[1], sb)
        own, other = grad_halves(expert_inputs, expert_grads, after(kept, step))
        step = (sb, back[1], back[4], back[5], other)

        for n, k in enumerate((2, 3, 6, 7)):
            back[k] = flip(after(rb[n * c : (n + 1) * c], step), "expert", k, f"returned_{k}")
        own, other = after((own, other), step)
        grads = grad_totals(own, flip(other, "dp", 1, "weight_grads"))
        grad_inputs = sum(
            by_rows(after(pick(filled, ks), needed), jnp.concatenate([back[k] for k in ks], axis=0))
            for ks, needed in (((0, 1, 4, 5), ()), ((2, 3, 6, 7), grads))
        ).astype(BF16)
    else:
        def exchange(rows):
            got = lax.all_to_all(
                rows.reshape(expert_count, capacity, features), "expert", split_axis=0, concat_axis=0, tiled=True
            )
            return got.reshape(-1, features)

        gate_weight, up_weight, down_weight = join_weights(*(flip(w[0], "dp", 1) for w in (w_gate, w_up, w_down)))
        beside = flip(jnp.concatenate([teacher, across], axis=0), "dp", 1)
        partner_teacher = partner_rows(teacher, across, beside, partner)
        aligned = jnp.dot(alignment, partner_teacher, preferred_element_type=F32)
        cotangent = (layer_out.astype(F32) - aligned).astype(BF16)
        x_rows = exchange(spread(filled.reshape(-1, tok_rows), inputs))
        g_rows = exchange(spread(weighted.reshape(-1, tok_rows), cotangent))
        expert_inputs = [both(x_rows, flip(x_rows, "dp", 2))]
        expert_grads = [both(g_rows, flip(g_rows, "dp", 2))]
        one, own, other = expert_rows(expert_inputs[0], x_rows.shape[0], expert_grads[0])
        kept = [one]
        back = exchange(total(own, flip(other, "dp", 2)))
        grad_inputs = by_rows(filled.reshape(-1, tok_rows), back).astype(BF16)
        own, other = grad_halves(expert_inputs, expert_grads, kept)
        grads = grad_totals(own, flip(other, "dp", 1))
    return grad_inputs, *grads


def solution(mesh):
    tokens = P(("expert", "dp"), None)
    columns, rows = P("expert", None, "dp"), P("expert", "dp", None)
    return jax.shard_map(
        per_device,
        mesh=mesh,
        in_specs=(tokens,) * 6 + (P(("expert", "dp")), columns, columns, rows),
        out_specs=(tokens, columns, columns, rows),
        check_vma=False,
    )
```

```python
import jax
import jax.numpy as jnp
import numpy as np
from jax import lax
from jax.sharding import PartitionSpec as P

F32, BF16 = jnp.float32, jnp.bfloat16


def flip(block, axis, shift, name="rows"):
    with jax.named_scope(name):
        return lax.ppermute(block, axis, [(i, i ^ shift) for i in range(lax.axis_size(axis))])


def by_columns(left, right):
    return lax.dot_general(left, right, (((1,), (1,)), ((), ())), preferred_element_type=F32)


def by_rows(left, right):
    return lax.dot_general(left, right, (((0,), (0,)), ((), ())), preferred_element_type=F32)


def slot_weights(filled, routes, route_weights, experts):
    named = routes.T[None] == experts[:, None, None]
    weight = jnp.sum(jnp.where(named, route_weights.T[None].astype(F32), 0.0), axis=1)
    return filled * weight[:, None, :].astype(BF16)


def slot_matrices(routes, experts, capacity):
    named = routes.T[None] == experts[:, None, None]
    member = jnp.any(named, axis=1)
    tokens = routes.shape[0]
    before = jnp.arange(tokens)[:, None] < jnp.arange(tokens)[None, :]
    earlier = jnp.dot(member.astype(BF16), before.astype(BF16), preferred_element_type=F32)
    slots = jnp.arange(capacity, dtype=F32)[None, :, None]
    filled = member[:, None, :] & (earlier[:, None, :] == slots)
    return filled.astype(BF16)


def after(block, *earlier):
    return lax.optimization_barrier((block, earlier))[0]


def partner_rows(teacher, across, beside, partner):
    tok_rows = teacher.shape[0]
    apart = partner[0] ^ lax.axis_index("dp")
    return jnp.where(
        apart < 2,
        jnp.where(apart == 0, teacher, beside[:tok_rows]),
        jnp.where(apart == 2, across, beside[tok_rows:]),
    )


def spread(matrices, rows):
    return jnp.dot(matrices, rows, preferred_element_type=F32).astype(BF16)


def grad_halves(inputs, grads, kept):
    inputs, grads = jnp.concatenate(inputs, axis=0), jnp.concatenate(grads, axis=0)
    hidden, d_gate, d_up = (jnp.concatenate(parts, axis=0) for parts in zip(*kept))
    quarter = hidden.shape[1] // 2
    own, other = slice(0, quarter), slice(quarter, None)
    side = by_rows(jnp.concatenate([d_gate[:, other], d_up[:, other]], axis=1), inputs).astype(BF16)
    down = by_rows(hidden[:, other], grads).astype(BF16)
    return (
        ((d_gate[:, own], inputs), (d_up[:, own], inputs), (hidden[:, own], grads)),
        jnp.concatenate([side, down], axis=0),
    )


def grad_totals(own, other):
    parts = jnp.split(other, 3, axis=0)
    gate, up, down = ((by_rows(*mine) + part.astype(F32)).astype(BF16) for mine, part in zip(own, parts))
    return gate.T[None], up.T[None], down[None]


def per_device(
    inputs, layer_out, teacher, alignment, routes, route_weights, partner, w_gate, w_up, w_down
):
    tok_rows, features = inputs.shape
    route_count = routes.shape[1]
    expert_count = lax.axis_size("expert")
    capacity = max(2, (5 * tok_rows * route_count + 4 * expert_count - 1) // (4 * expert_count))
    me = lax.axis_index("expert")
    quarter = w_gate.shape[2]
    small = expert_count == 8

    across = flip(teacher, "dp", 2, "teacher_across")

    experts = jnp.arange(expert_count, dtype=jnp.int32)
    experts = experts ^ me if small else experts
    filled = slot_matrices(routes, experts, capacity)
    weighted = slot_weights(filled, routes, after(route_weights, across), experts)

    def pick(matrices, shifts):
        return jnp.concatenate([matrices[k] for k in shifts], axis=0)

    def expert_rows(rows, half, grads):
        gate_term = jnp.dot(rows, gate_weight, preferred_element_type=F32)
        up_term = jnp.dot(rows, up_weight, preferred_element_type=F32)
        sigmoid_gate = jax.nn.sigmoid(gate_term)
        activated = gate_term * sigmoid_gate
        hidden = (activated * up_term).astype(BF16)
        d_hidden = by_columns(grads, down_weight)
        d_gate = (d_hidden * up_term * (sigmoid_gate + activated * (1.0 - sigmoid_gate))).astype(BF16)
        d_up = (d_hidden * activated).astype(BF16)
        sums = by_columns(d_gate, gate_weight) + by_columns(d_up, up_weight)
        return (hidden, d_gate, d_up), sums[:half], sums[half:].astype(BF16)

    def both(rows, other):
        return jnp.concatenate([rows, other], axis=0)

    def total(own, other):
        return (own + other.astype(F32)).astype(BF16)

    def join_weights(gate_other, up_other, down_other):
        return (
            jnp.concatenate([w_gate[0], gate_other], axis=1),
            jnp.concatenate([w_up[0], up_other], axis=1),
            jnp.concatenate([w_down[0], down_other], axis=0),
        )

    if small:
        c = capacity

        sent = [spread(pick(filled, (1, 3, 7)), inputs)] + [spread(filled[k], inputs) for k in (4, 5)]
        sent = lax.optimization_barrier(sent)
        x_side = flip(sent[0], "expert", 1, "inputs_side")
        x_far = [flip(rows, "expert", k, f"inputs_far_{k}") for k, rows in zip((4, 5), sent[1:])]
        beside = flip(jnp.concatenate([teacher, across], axis=0), "dp", 1, "teacher_beside")

        x_own, near2, near6 = [spread(after(filled[k], across), inputs) for k in (0, 2, 6)]
        xa = jnp.concatenate([x_own, x_side[:c]] + x_far, axis=0)
        partner_teacher = partner_rows(teacher, across, beside, partner)
        aligned = jnp.dot(alignment, partner_teacher, preferred_element_type=F32)
        cotangent = (layer_out.astype(F32) - aligned).astype(BF16)
        g_send = spread(pick(weighted, (1, 3, 5, 7)), cotangent)
        g_side = flip(g_send, "expert", 1, "grads_side")
        ya = flip(after(xa, g_send), "dp", 2, "inputs_a")
        x_z3 = flip(after(jnp.concatenate([near6, x_side[2 * c :]], axis=0), x_far, g_send), "expert", 6, "inputs_z3")
        x_z1 = flip(after(jnp.concatenate([near2, x_side[c : 2 * c]], axis=0), x_far, g_send), "expert", 2, "inputs_z1")
        g_own, gear2, gear4, gear6 = [spread(weighted[k], cotangent) for k in (0, 2, 4, 6)]
        gate_other = flip(after(w_gate[0], cotangent), "dp", 1, "gate_weight")
        xb = jnp.concatenate([x_z1, x_z3], axis=0)

        yb = flip(after(xb, ya, g_side), "dp", 2, "inputs_b")
        g_z2 = flip(after(jnp.concatenate([gear4, g_side[2 * c : 3 * c]], axis=0), x_z3, x_z1), "expert", 4, "grads_z2")
        g_z1 = flip(after(jnp.concatenate([gear2, g_side[c : 2 * c]], axis=0), x_z3, x_z1), "expert", 2, "grads_z1")
        up_other = flip(after(w_up[0], gate_other, x_z3), "dp", 1, "up_weight")

        ga = jnp.concatenate([g_own, g_side[:c], g_z2], axis=0)
        ha = flip(after(ga, yb), "dp", 2, "grads_a")
        g_z3 = flip(after(jnp.concatenate([gear6, g_side[3 * c :]], axis=0), g_z2), "expert", 6, "grads_z3")
        down_other = flip(after(w_down[0], up_other, yb), "dp", 1, "down_weight")
        gate_weight, up_weight, down_weight = join_weights(gate_other, up_other, down_other)

        gb = jnp.concatenate([g_z1, g_z3], axis=0)
        hb = flip(after(gb, ha, down_other), "dp", 2, "grads_b")
        expert_inputs = [both(xa, ya), both(xb, yb)]
        expert_grads = [both(ga, ha), both(gb, hb)]
        kept, own_sums, other_sums = zip(
            *[expert_rows(r, r.shape[0] // 2, g) for r, g in zip(expert_inputs, expert_grads)]
        )

        sa = flip(after(other_sums[0], hb), "dp", 2, "sums_a")
        ra = total(own_sums[0], sa)

        step = (sa, other_sums[1])
        sb = flip(after(other_sums[1], step), "dp", 2, "sums_b")
        back = {0: ra[:c]}
        for n, k in enumerate((1, 4, 5), 1):
            back[k] = flip(after(ra[n * c : (n + 1) * c], step), "expert", k, f"returned_{k}")
        rb = total(own_sums[1], sb)
        own, other = grad_halves(expert_inputs, expert_grads, after(kept, step))
        step = (sb, back[1], back[4], back[5], other)

        for n, k in enumerate((2, 3, 6, 7)):
            back[k] = flip(after(rb[n * c : (n + 1) * c], step), "expert", k, f"returned_{k}")
        own, other = after((own, other), step)
        grads = grad_totals(own, flip(other, "dp", 1, "weight_grads"))
        grad_inputs = sum(
            by_rows(after(pick(filled, ks), needed), jnp.concatenate([back[k] for k in ks], axis=0))
            for ks, needed in (((0, 1, 4, 5), ()), ((2, 3, 6, 7), grads))
        ).astype(BF16)
    else:
        def exchange(rows):
            got = lax.all_to_all(
                rows.reshape(expert_count, capacity, features), "expert", split_axis=0, concat_axis=0, tiled=True
            )
            return got.reshape(-1, features)

        gate_weight, up_weight, down_weight = join_weights(*(flip(w[0], "dp", 1) for w in (w_gate, w_up, w_down)))
        beside = flip(jnp.concatenate([teacher, across], axis=0), "dp", 1)
        partner_teacher = partner_rows(teacher, across, beside, partner)
        aligned = jnp.dot(alignment, partner_teacher, preferred_element_type=F32)
        cotangent = (layer_out.astype(F32) - aligned).astype(BF16)
        x_rows = exchange(spread(filled.reshape(-1, tok_rows), inputs))
        g_rows = exchange(spread(weighted.reshape(-1, tok_rows), cotangent))
        expert_inputs = [both(x_rows, flip(x_rows, "dp", 2))]
        expert_grads = [both(g_rows, flip(g_rows, "dp", 2))]
        one, own, other = expert_rows(expert_inputs[0], x_rows.shape[0], expert_grads[0])
        kept = [one]
        back = exchange(total(own, flip(other, "dp", 2)))
        grad_inputs = by_rows(filled.reshape(-1, tok_rows), back).astype(BF16)
        own, other = grad_halves(expert_inputs, expert_grads, kept)
        grads = grad_totals(own, flip(other, "dp", 1))
    return grad_inputs, *grads


def solution(mesh):
    tokens = P(("expert", "dp"), None)
    columns, rows = P("expert", None, "dp"), P("expert", "dp", None)
    return jax.shard_map(
        per_device,
        mesh=mesh,
        in_specs=(tokens,) * 6 + (P(("expert", "dp")), columns, columns, rows),
        out_specs=(tokens, columns, columns, rows),
        check_vma=False,
    )
```

```python
import jax
import jax.numpy as jnp
import numpy as np
from jax import lax
from jax.sharding import PartitionSpec as P

F32, BF16 = jnp.float32, jnp.bfloat16


def flip(block, axis, shift, name="rows"):
    with jax.named_scope(name):
        return lax.ppermute(block, axis, [(i, i ^ shift) for i in range(lax.axis_size(axis))])


def by_columns(left, right):
    return lax.dot_general(left, right, (((1,), (1,)), ((), ())), preferred_element_type=F32)


def by_rows(left, right):
    return lax.dot_general(left, right, (((0,), (0,)), ((), ())), preferred_element_type=F32)


def slot_weights(filled, routes, route_weights, experts):
    named = routes.T[None] == experts[:, None, None]
    weight = jnp.sum(jnp.where(named, route_weights.T[None].astype(F32), 0.0), axis=1)
    return filled * weight[:, None, :].astype(BF16)


def slot_matrices(routes, experts, capacity):
    named = routes.T[None] == experts[:, None, None]
    member = jnp.any(named, axis=1)
    tokens = routes.shape[0]
    before = jnp.arange(tokens)[:, None] < jnp.arange(tokens)[None, :]
    earlier = jnp.dot(member.astype(BF16), before.astype(BF16), preferred_element_type=F32)
    slots = jnp.arange(capacity, dtype=F32)[None, :, None]
    filled = member[:, None, :] & (earlier[:, None, :] == slots)
    return filled.astype(BF16)


def after(block, *earlier):
    return lax.optimization_barrier((block, earlier))[0]


def partner_rows(teacher, across, beside, partner):
    tok_rows = teacher.shape[0]
    apart = partner[0] ^ lax.axis_index("dp")
    return jnp.where(
        apart < 2,
        jnp.where(apart == 0, teacher, beside[:tok_rows]),
        jnp.where(apart == 2, across, beside[tok_rows:]),
    )


def spread(matrices, rows):
    return jnp.dot(matrices, rows, preferred_element_type=F32).astype(BF16)


def grad_halves(inputs, grads, kept):
    inputs, grads = jnp.concatenate(inputs, axis=0), jnp.concatenate(grads, axis=0)
    hidden, d_gate, d_up = (jnp.concatenate(parts, axis=0) for parts in zip(*kept))
    quarter = hidden.shape[1] // 2
    own, other = slice(0, quarter), slice(quarter, None)
    side = by_rows(jnp.concatenate([d_gate[:, other], d_up[:, other]], axis=1), inputs).astype(BF16)
    down = by_rows(hidden[:, other], grads).astype(BF16)
    return (
        ((d_gate[:, own], inputs), (d_up[:, own], inputs), (hidden[:, own], grads)),
        jnp.concatenate([side, down], axis=0),
    )


def grad_totals(own, other):
    parts = jnp.split(other, 3, axis=0)
    gate, up, down = ((by_rows(*mine) + part.astype(F32)).astype(BF16) for mine, part in zip(own, parts))
    return gate.T[None], up.T[None], down[None]


def per_device(
    inputs, layer_out, teacher, alignment, routes, route_weights, partner, w_gate, w_up, w_down
):
    tok_rows, features = inputs.shape
    route_count = routes.shape[1]
    expert_count = lax.axis_size("expert")
    capacity = max(2, (5 * tok_rows * route_count + 4 * expert_count - 1) // (4 * expert_count))
    me = lax.axis_index("expert")
    quarter = w_gate.shape[2]
    small = expert_count == 8

    across = flip(teacher, "dp", 2, "teacher_across")

    experts = jnp.arange(expert_count, dtype=jnp.int32)
    experts = experts ^ me if small else experts
    filled = slot_matrices(routes, experts, capacity)

    def pick(matrices, shifts):
        return jnp.concatenate([matrices[k] for k in shifts], axis=0)

    def expert_rows(rows, half, grads):
        gate_term = jnp.dot(rows, gate_weight, preferred_element_type=F32)
        up_term = jnp.dot(rows, up_weight, preferred_element_type=F32)
        sigmoid_gate = jax.nn.sigmoid(gate_term)
        activated = gate_term * sigmoid_gate
        hidden = (activated * up_term).astype(BF16)
        d_hidden = by_columns(grads, down_weight)
        d_gate = (d_hidden * up_term * (sigmoid_gate + activated * (1.0 - sigmoid_gate))).astype(BF16)
        d_up = (d_hidden * activated).astype(BF16)
        sums = by_columns(d_gate, gate_weight) + by_columns(d_up, up_weight)
        return (hidden, d_gate, d_up), sums[:half], sums[half:].astype(BF16)

    def both(rows, other):
        return jnp.concatenate([rows, other], axis=0)

    def total(own, other):
        return (own + other.astype(F32)).astype(BF16)

    def join_weights(gate_other, up_other, down_other):
        return (
            jnp.concatenate([w_gate[0], gate_other], axis=1),
            jnp.concatenate([w_up[0], up_other], axis=1),
            jnp.concatenate([w_down[0], down_other], axis=0),
        )

    if small:
        c = capacity

        sent = [spread(pick(filled, (1, 3, 7)), inputs)]
        for k in (4, 5):
            sent.append(spread(after(filled[k], sent[-1]), inputs))
        weighted = slot_weights(filled, routes, after(route_weights, sent[0]), experts)
        gate_other = flip(w_gate[0], "dp", 1, "gate_weight")
        up_other = flip(after(w_up[0], gate_other), "dp", 1, "up_weight")
        x_side = flip(sent[0], "expert", 1, "inputs_side")
        x_far = [flip(rows, "expert", k, f"inputs_far_{k}") for k, rows in zip((4, 5), sent[1:])]
        beside = flip(after(jnp.concatenate([teacher, across], axis=0), gate_other), "dp", 1, "teacher_beside")

        x_own, near2, near6 = [spread(after(filled[k], across), inputs) for k in (0, 2, 6)]
        partner_teacher = partner_rows(teacher, across, beside, partner)
        aligned = jnp.dot(alignment, partner_teacher, preferred_element_type=F32)
        cotangent = (layer_out.astype(F32) - aligned).astype(BF16)
        g_send = spread(pick(weighted, (1, 3, 5, 7)), cotangent)
        xa = jnp.concatenate(after([x_own, x_side[:c]] + x_far, g_send), axis=0)
        g_side = flip(g_send, "expert", 1, "grads_side")
        ya = flip(xa, "dp", 2, "inputs_a")
        x_z3 = flip(after(jnp.concatenate([near6, x_side[2 * c :]], axis=0), x_far, g_send), "expert", 6, "inputs_z3")
        x_z1 = flip(after(jnp.concatenate([near2, x_side[c : 2 * c]], axis=0), x_far, g_send), "expert", 2, "inputs_z1")
        g_own, gear2, gear4, gear6 = [spread(weighted[k], cotangent) for k in (0, 2, 4, 6)]
        xb = jnp.concatenate([x_z1, x_z3], axis=0)

        down_other = flip(after(w_down[0], cotangent), "dp", 1, "down_weight")
        gate_weight, up_weight, down_weight = join_weights(gate_other, up_other, down_other)

        yb = flip(after(xb, g_side), "dp", 2, "inputs_b")
        g_z2 = flip(after(jnp.concatenate([gear4, g_side[2 * c : 3 * c]], axis=0), x_z3, x_z1), "expert", 4, "grads_z2")
        g_z1 = flip(after(jnp.concatenate([gear2, g_side[c : 2 * c]], axis=0), x_z3, x_z1), "expert", 2, "grads_z1")

        ga = jnp.concatenate([g_own, g_side[:c], g_z2], axis=0)
        ha = flip(ga, "dp", 2, "grads_a")
        g_z3 = flip(after(jnp.concatenate([gear6, g_side[3 * c :]], axis=0), g_z2), "expert", 6, "grads_z3")

        gb = jnp.concatenate([g_z1, g_z3], axis=0)
        hb = flip(gb, "dp", 2, "grads_b")
        expert_inputs = [both(xa, ya), both(xb, yb)]
        expert_grads = [both(ga, ha), both(gb, hb)]
        kept, own_sums, other_sums = zip(
            *[expert_rows(r, r.shape[0] // 2, g) for r, g in zip(expert_inputs, expert_grads)]
        )

        sa = flip(other_sums[0], "dp", 2, "sums_a")
        ra = total(own_sums[0], sa)

        step = (sa, other_sums[1])
        sb = flip(other_sums[1], "dp", 2, "sums_b")
        back = {0: ra[:c]}
        for n, k in enumerate((1, 4, 5), 1):
            back[k] = flip(ra[n * c : (n + 1) * c], "expert", k, f"returned_{k}")
        rb = total(own_sums[1], sb)
        own, other = grad_halves(expert_inputs, expert_grads, after(kept, step))
        step = (sb, back[1], back[4], back[5], other)

        for n, k in enumerate((2, 3, 6, 7)):
            back[k] = flip(after(rb[n * c : (n + 1) * c], step), "expert", k, f"returned_{k}")
        own, other = after((own, other), step)
        grads = grad_totals(own, flip(other, "dp", 1, "weight_grads"))
        grad_inputs = sum(
            by_rows(after(pick(filled, ks), needed), jnp.concatenate([back[k] for k in ks], axis=0))
            for ks, needed in (((0, 1, 4, 5), ()), ((2, 3, 6, 7), grads))
        ).astype(BF16)
    else:
        weighted = slot_weights(filled, routes, route_weights, experts)

        def exchange(rows):
            got = lax.all_to_all(
                rows.reshape(expert_count, capacity, features), "expert", split_axis=0, concat_axis=0, tiled=True
            )
            return got.reshape(-1, features)

        gate_weight, up_weight, down_weight = join_weights(*(flip(w[0], "dp", 1) for w in (w_gate, w_up, w_down)))
        beside = flip(jnp.concatenate([teacher, across], axis=0), "dp", 1)
        partner_teacher = partner_rows(teacher, across, beside, partner)
        aligned = jnp.dot(alignment, partner_teacher, preferred_element_type=F32)
        cotangent = (layer_out.astype(F32) - aligned).astype(BF16)
        x_rows = exchange(spread(filled.reshape(-1, tok_rows), inputs))
        g_rows = exchange(spread(weighted.reshape(-1, tok_rows), cotangent))
        expert_inputs = [both(x_rows, flip(x_rows, "dp", 2))]
        expert_grads = [both(g_rows, flip(g_rows, "dp", 2))]
        one, own, other = expert_rows(expert_inputs[0], x_rows.shape[0], expert_grads[0])
        kept = [one]
        back = exchange(total(own, flip(other, "dp", 2)))
        grad_inputs = by_rows(filled.reshape(-1, tok_rows), back).astype(BF16)
        own, other = grad_halves(expert_inputs, expert_grads, kept)
        grads = grad_totals(own, flip(other, "dp", 1))
    return grad_inputs, *grads


def solution(mesh):
    tokens = P(("expert", "dp"), None)
    columns, rows = P("expert", None, "dp"), P("expert", "dp", None)
    return jax.shard_map(
        per_device,
        mesh=mesh,
        in_specs=(tokens,) * 6 + (P(("expert", "dp")), columns, columns, rows),
        out_specs=(tokens, columns, columns, rows),
        check_vma=False,
    )
```

```python
import jax
import jax.numpy as jnp
import numpy as np
from jax import lax
from jax.sharding import PartitionSpec as P

F32, BF16 = jnp.float32, jnp.bfloat16


def flip(block, axis, shift, name="rows"):
    with jax.named_scope(name):
        return lax.ppermute(block, axis, [(i, i ^ shift) for i in range(lax.axis_size(axis))])


def by_columns(left, right):
    return lax.dot_general(left, right, (((1,), (1,)), ((), ())), preferred_element_type=F32)


def by_rows(left, right):
    return lax.dot_general(left, right, (((0,), (0,)), ((), ())), preferred_element_type=F32)


def slot_weights(filled, routes, route_weights, experts):
    named = routes.T[None] == experts[:, None, None]
    weight = jnp.sum(jnp.where(named, route_weights.T[None].astype(F32), 0.0), axis=1)
    return filled * weight[:, None, :].astype(BF16)


def slot_matrices(routes, experts, capacity):
    named = routes.T[None] == experts[:, None, None]
    member = jnp.any(named, axis=1)
    tokens = routes.shape[0]
    before = jnp.arange(tokens)[:, None] < jnp.arange(tokens)[None, :]
    earlier = jnp.dot(member.astype(BF16), before.astype(BF16), preferred_element_type=F32)
    slots = jnp.arange(capacity, dtype=F32)[None, :, None]
    filled = member[:, None, :] & (earlier[:, None, :] == slots)
    return filled.astype(BF16)


def after(block, *earlier):
    return lax.optimization_barrier((block, earlier))[0]


def partner_rows(teacher, across, beside, partner):
    tok_rows = teacher.shape[0]
    apart = partner[0] ^ lax.axis_index("dp")
    return jnp.where(
        apart < 2,
        jnp.where(apart == 0, teacher, beside[:tok_rows]),
        jnp.where(apart == 2, across, beside[tok_rows:]),
    )


def spread(matrices, rows):
    return jnp.dot(matrices, rows, preferred_element_type=F32).astype(BF16)


def grad_halves(inputs, grads, kept):
    inputs, grads = jnp.concatenate(inputs, axis=0), jnp.concatenate(grads, axis=0)
    hidden, d_gate, d_up = (jnp.concatenate(parts, axis=0) for parts in zip(*kept))
    quarter = hidden.shape[1] // 2
    own, other = slice(0, quarter), slice(quarter, None)
    side = by_rows(jnp.concatenate([d_gate[:, other], d_up[:, other]], axis=1), inputs).astype(BF16)
    down = by_rows(hidden[:, other], grads).astype(BF16)
    return (
        ((d_gate[:, own], inputs), (d_up[:, own], inputs), (hidden[:, own], grads)),
        jnp.concatenate([side, down], axis=0),
    )


def grad_totals(own, other):
    parts = jnp.split(other, 3, axis=0)
    gate, up, down = ((by_rows(*mine) + part.astype(F32)).astype(BF16) for mine, part in zip(own, parts))
    return gate.T[None], up.T[None], down[None]


def per_device(
    inputs, layer_out, teacher, alignment, routes, route_weights, partner, w_gate, w_up, w_down
):
    tok_rows, features = inputs.shape
    route_count = routes.shape[1]
    expert_count = lax.axis_size("expert")
    capacity = max(2, (5 * tok_rows * route_count + 4 * expert_count - 1) // (4 * expert_count))
    me = lax.axis_index("expert")
    quarter = w_gate.shape[2]
    small = expert_count == 8

    across = flip(teacher, "dp", 2, "teacher_across")

    experts = jnp.arange(expert_count, dtype=jnp.int32)
    experts = experts ^ me if small else experts
    filled = slot_matrices(routes, experts, capacity)

    def pick(matrices, shifts):
        return jnp.concatenate([matrices[k] for k in shifts], axis=0)

    def expert_rows(rows, half, grads):
        gate_term = jnp.dot(rows, gate_weight, preferred_element_type=F32)
        up_term = jnp.dot(rows, up_weight, preferred_element_type=F32)
        sigmoid_gate = jax.nn.sigmoid(gate_term)
        activated = gate_term * sigmoid_gate
        hidden = (activated * up_term).astype(BF16)
        d_hidden = by_columns(grads, down_weight)
        d_gate = (d_hidden * up_term * (sigmoid_gate + activated * (1.0 - sigmoid_gate))).astype(BF16)
        d_up = (d_hidden * activated).astype(BF16)
        sums = by_columns(d_gate, gate_weight) + by_columns(d_up, up_weight)
        return (hidden, d_gate, d_up), sums[:half], sums[half:].astype(BF16)

    def both(rows, other):
        return jnp.concatenate([rows, other], axis=0)

    def total(own, other):
        return (own + other.astype(F32)).astype(BF16)

    def join_weights(gate_other, up_other, down_other):
        return (
            jnp.concatenate([w_gate[0], gate_other], axis=1),
            jnp.concatenate([w_up[0], up_other], axis=1),
            jnp.concatenate([w_down[0], down_other], axis=0),
        )

    if small:
        c = capacity

        sent = [spread(pick(filled, (1, 3, 7)), inputs)]
        for k in (4, 5):
            sent.append(spread(after(filled[k], sent[-1]), inputs))
        weighted = slot_weights(filled, routes, after(route_weights, sent[0]), experts)
        gate_other = flip(w_gate[0], "dp", 1, "gate_weight")
        up_other = flip(after(w_up[0], gate_other), "dp", 1, "up_weight")
        x_side = flip(sent[0], "expert", 1, "inputs_side")
        x_far = [flip(rows, "expert", k, f"inputs_far_{k}") for k, rows in zip((4, 5), sent[1:])]
        beside = flip(after(jnp.concatenate([teacher, across], axis=0), gate_other), "dp", 1, "teacher_beside")

        x_own, near2, near6 = [spread(after(filled[k], across), inputs) for k in (0, 2, 6)]
        partner_teacher = partner_rows(teacher, across, beside, partner)
        aligned = jnp.dot(alignment, partner_teacher, preferred_element_type=F32)
        cotangent = (layer_out.astype(F32) - aligned).astype(BF16)
        g_send = spread(pick(weighted, (1, 3, 5, 7)), cotangent)
        xa = jnp.concatenate(after([x_own, x_side[:c]] + x_far, g_send), axis=0)
        g_side = flip(g_send, "expert", 1, "grads_side")
        ya = flip(xa, "dp", 2, "inputs_a")
        x_z3 = flip(after(jnp.concatenate([near6, x_side[2 * c :]], axis=0), x_far, g_send), "expert", 6, "inputs_z3")
        x_z1 = flip(after(jnp.concatenate([near2, x_side[c : 2 * c]], axis=0), x_far, g_send), "expert", 2, "inputs_z1")
        g_own, gear2, gear4, gear6 = [spread(weighted[k], cotangent) for k in (0, 2, 4, 6)]
        xb = jnp.concatenate([x_z1, x_z3], axis=0)

        down_other = flip(after(w_down[0], cotangent), "dp", 1, "down_weight")
        gate_weight, up_weight, down_weight = join_weights(gate_other, up_other, down_other)

        yb = flip(after(xb, g_side), "dp", 2, "inputs_b")
        g_z2 = flip(after(jnp.concatenate([gear4, g_side[2 * c : 3 * c]], axis=0), x_z3, x_z1), "expert", 4, "grads_z2")
        g_z1 = flip(after(jnp.concatenate([gear2, g_side[c : 2 * c]], axis=0), x_z3, x_z1), "expert", 2, "grads_z1")

        ga = jnp.concatenate([g_own, g_side[:c], g_z2], axis=0)
        ha = flip(ga, "dp", 2, "grads_a")
        g_z3 = flip(after(jnp.concatenate([gear6, g_side[3 * c :]], axis=0), ga), "expert", 6, "grads_z3")

        gb = jnp.concatenate([g_z1, g_z3], axis=0)
        hb = flip(gb, "dp", 2, "grads_b")
        expert_inputs = [both(xa, ya), both(xb, yb)]
        expert_grads = [both(ga, ha), both(gb, hb)]
        kept, own_sums, other_sums = zip(
            *[expert_rows(r, r.shape[0] // 2, g) for r, g in zip(expert_inputs, expert_grads)]
        )

        s_z2 = flip(other_sums[0][2 * c :], "dp", 2, "sums_z2")
        r_z2 = total(own_sums[0][2 * c :], s_z2)
        s_z3 = flip(other_sums[1][2 * c :], "dp", 2, "sums_z3")
        r_z3 = total(own_sums[1][2 * c :], s_z3)
        s_near = jnp.concatenate([other_sums[0][: 2 * c], other_sums[1][: 2 * c]], axis=0)
        s_near = flip(after(s_near, s_z3, s_z2), "dp", 2, "sums_near")
        s_near = after(s_near, r_z2, r_z3)
        r_near = [total(own_sums[n][: 2 * c], s_near[2 * n * c : 2 * (n + 1) * c]) for n in range(2)]
        back = {0: r_near[0][:c]}
        for rows, first in ((r_z2, 4), (r_z3, 6)):
            for n in range(2):
                back[first + n] = flip(rows[n * c : (n + 1) * c], "expert", first + n, f"R{first + n}")
        own, other = grad_halves(expert_inputs, expert_grads, after(kept, other_sums[1]))
        other = flip(after(other, back[4], back[5], s_near), "dp", 1, "weight_grads")
        for rows, k in ((r_near[0][c:], 1), (r_near[1][:c], 2), (r_near[1][c:], 3)):
            back[k] = flip(after(rows, back[4], back[5]), "expert", k, f"returned_{k}")
        grads = grad_totals(own, other)
        grad_inputs = sum(
            by_rows(after(pick(filled, ks), needed), jnp.concatenate([back[k] for k in ks], axis=0))
            for ks, needed in (((0, 1, 4, 5), ()), ((2, 3, 6, 7), grads))
        ).astype(BF16)
    else:
        weighted = slot_weights(filled, routes, route_weights, experts)

        def exchange(rows):
            got = lax.all_to_all(
                rows.reshape(expert_count, capacity, features), "expert", split_axis=0, concat_axis=0, tiled=True
            )
            return got.reshape(-1, features)

        gate_weight, up_weight, down_weight = join_weights(*(flip(w[0], "dp", 1) for w in (w_gate, w_up, w_down)))
        beside = flip(jnp.concatenate([teacher, across], axis=0), "dp", 1)
        partner_teacher = partner_rows(teacher, across, beside, partner)
        aligned = jnp.dot(alignment, partner_teacher, preferred_element_type=F32)
        cotangent = (layer_out.astype(F32) - aligned).astype(BF16)
        x_rows = exchange(spread(filled.reshape(-1, tok_rows), inputs))
        g_rows = exchange(spread(weighted.reshape(-1, tok_rows), cotangent))
        expert_inputs = [both(x_rows, flip(x_rows, "dp", 2))]
        expert_grads = [both(g_rows, flip(g_rows, "dp", 2))]
        one, own, other = expert_rows(expert_inputs[0], x_rows.shape[0], expert_grads[0])
        kept = [one]
        back = exchange(total(own, flip(other, "dp", 2)))
        grad_inputs = by_rows(filled.reshape(-1, tok_rows), back).astype(BF16)
        own, other = grad_halves(expert_inputs, expert_grads, kept)
        grads = grad_totals(own, flip(other, "dp", 1))
    return grad_inputs, *grads


def solution(mesh):
    tokens = P(("expert", "dp"), None)
    columns, rows = P("expert", None, "dp"), P("expert", "dp", None)
    return jax.shard_map(
        per_device,
        mesh=mesh,
        in_specs=(tokens,) * 6 + (P(("expert", "dp")), columns, columns, rows),
        out_specs=(tokens, columns, columns, rows),
        check_vma=False,
    )
```

```python
import jax
import jax.numpy as jnp
import numpy as np
from jax import lax
from jax.sharding import PartitionSpec as P

F32, BF16 = jnp.float32, jnp.bfloat16


def flip(block, axis, shift, name="rows"):
    with jax.named_scope(name):
        return lax.ppermute(block, axis, [(i, i ^ shift) for i in range(lax.axis_size(axis))])


def by_columns(left, right):
    return lax.dot_general(left, right, (((1,), (1,)), ((), ())), preferred_element_type=F32)


def by_rows(left, right):
    return lax.dot_general(left, right, (((0,), (0,)), ((), ())), preferred_element_type=F32)


def slot_weights(filled, routes, route_weights, experts):
    named = routes.T[None] == experts[:, None, None]
    weight = jnp.sum(jnp.where(named, route_weights.T[None].astype(F32), 0.0), axis=1)
    return filled * weight[:, None, :].astype(BF16)


def slot_matrices(routes, experts, capacity):
    named = routes.T[None] == experts[:, None, None]
    member = jnp.any(named, axis=1)
    tokens = routes.shape[0]
    before = jnp.arange(tokens)[:, None] < jnp.arange(tokens)[None, :]
    earlier = jnp.dot(member.astype(BF16), before.astype(BF16), preferred_element_type=F32)
    slots = jnp.arange(capacity, dtype=F32)[None, :, None]
    filled = member[:, None, :] & (earlier[:, None, :] == slots)
    return filled.astype(BF16)


def after(block, *earlier):
    return lax.optimization_barrier((block, earlier))[0]


def partner_rows(teacher, across, beside, partner):
    tok_rows = teacher.shape[0]
    apart = partner[0] ^ lax.axis_index("dp")
    return jnp.where(
        apart < 2,
        jnp.where(apart == 0, teacher, beside[:tok_rows]),
        jnp.where(apart == 2, across, beside[tok_rows:]),
    )


def spread(matrices, rows):
    return jnp.dot(matrices, rows, preferred_element_type=F32).astype(BF16)


def grad_halves(inputs, grads, kept):
    inputs, grads = jnp.concatenate(inputs, axis=0), jnp.concatenate(grads, axis=0)
    hidden, d_gate, d_up = (jnp.concatenate(parts, axis=0) for parts in zip(*kept))
    quarter = hidden.shape[1] // 2
    own, other = slice(0, quarter), slice(quarter, None)
    side = by_rows(jnp.concatenate([d_gate[:, other], d_up[:, other]], axis=1), inputs).astype(BF16)
    down = by_rows(hidden[:, other], grads).astype(BF16)
    return (
        ((d_gate[:, own], inputs), (d_up[:, own], inputs), (hidden[:, own], grads)),
        jnp.concatenate([side, down], axis=0),
    )


def grad_totals(own, other):
    parts = jnp.split(other, 3, axis=0)
    gate, up, down = ((by_rows(*mine) + part.astype(F32)).astype(BF16) for mine, part in zip(own, parts))
    return gate.T[None], up.T[None], down[None]


def per_device(
    inputs, layer_out, teacher, alignment, routes, route_weights, partner, w_gate, w_up, w_down
):
    tok_rows, features = inputs.shape
    route_count = routes.shape[1]
    expert_count = lax.axis_size("expert")
    capacity = max(2, (5 * tok_rows * route_count + 4 * expert_count - 1) // (4 * expert_count))
    me = lax.axis_index("expert")
    quarter = w_gate.shape[2]
    small = expert_count == 8

    across = flip(teacher, "dp", 2, "teacher_across")

    experts = jnp.arange(expert_count, dtype=jnp.int32)
    experts = experts ^ me if small else experts
    filled = slot_matrices(routes, experts, capacity)

    def pick(matrices, shifts):
        return jnp.concatenate([matrices[k] for k in shifts], axis=0)

    def expert_rows(rows, half, grads):
        gate_term = jnp.dot(rows, gate_weight, preferred_element_type=F32)
        up_term = jnp.dot(rows, up_weight, preferred_element_type=F32)
        sigmoid_gate = jax.nn.sigmoid(gate_term)
        activated = gate_term * sigmoid_gate
        hidden = (activated * up_term).astype(BF16)
        d_hidden = by_columns(grads, down_weight)
        d_gate = (d_hidden * up_term * (sigmoid_gate + activated * (1.0 - sigmoid_gate))).astype(BF16)
        d_up = (d_hidden * activated).astype(BF16)
        sums = by_columns(d_gate, gate_weight) + by_columns(d_up, up_weight)
        return (hidden, d_gate, d_up), sums[:half], sums[half:].astype(BF16)

    def both(rows, other):
        return jnp.concatenate([rows, other], axis=0)

    def total(own, other):
        return (own + other.astype(F32)).astype(BF16)

    def join_weights(gate_other, up_other, down_other):
        return (
            jnp.concatenate([w_gate[0], gate_other], axis=1),
            jnp.concatenate([w_up[0], up_other], axis=1),
            jnp.concatenate([w_down[0], down_other], axis=0),
        )

    if small:
        c = capacity

        sent = [spread(pick(filled, (1, 3, 7)), inputs)]
        for k in (4, 5):
            sent.append(spread(after(filled[k], sent[-1]), inputs))
        weighted = slot_weights(filled, routes, after(route_weights, sent[0]), experts)
        gate_other = flip(w_gate[0], "dp", 1, "gate_weight")
        up_other = flip(after(w_up[0], gate_other), "dp", 1, "up_weight")
        x_side = flip(sent[0], "expert", 1, "inputs_side")
        x_far = [flip(rows, "expert", k, f"inputs_far_{k}") for k, rows in zip((4, 5), sent[1:])]
        beside = flip(after(jnp.concatenate([teacher, across], axis=0), gate_other), "dp", 1, "teacher_beside")

        x_own, near2, near6 = [spread(after(filled[k], across), inputs) for k in (0, 2, 6)]
        partner_teacher = partner_rows(teacher, across, beside, partner)
        aligned = jnp.dot(alignment, partner_teacher, preferred_element_type=F32)
        cotangent = (layer_out.astype(F32) - aligned).astype(BF16)
        g_send = spread(pick(weighted, (1, 3, 5, 7)), cotangent)
        xa = jnp.concatenate(after([x_own, x_side[:c]] + x_far, g_send), axis=0)
        g_side = flip(g_send, "expert", 1, "grads_side")
        ya = flip(xa, "dp", 2, "inputs_a")
        x_z3 = flip(after(jnp.concatenate([near6, x_side[2 * c :]], axis=0), g_send), "expert", 6, "inputs_z3")
        x_z1 = flip(after(jnp.concatenate([near2, x_side[c : 2 * c]], axis=0), g_send), "expert", 2, "inputs_z1")
        g_own, gear2, gear4, gear6 = [spread(weighted[k], cotangent) for k in (0, 2, 4, 6)]
        xb = jnp.concatenate([x_z1, x_z3], axis=0)

        down_other = flip(after(w_down[0], cotangent), "dp", 1, "down_weight")
        gate_weight, up_weight, down_weight = join_weights(gate_other, up_other, down_other)

        yb = flip(after(xb, g_side), "dp", 2, "inputs_b")
        g_z2 = flip(after(jnp.concatenate([gear4, g_side[2 * c : 3 * c]], axis=0), x_z3, x_z1), "expert", 4, "grads_z2")
        g_z1 = flip(after(jnp.concatenate([gear2, g_side[c : 2 * c]], axis=0), x_z3, x_z1), "expert", 2, "grads_z1")

        ga = jnp.concatenate([g_own, g_side[:c], g_z2], axis=0)
        ha = flip(ga, "dp", 2, "grads_a")
        g_z3 = flip(after(jnp.concatenate([gear6, g_side[3 * c :]], axis=0), ga), "expert", 6, "grads_z3")

        gb = jnp.concatenate([g_z1, g_z3], axis=0)
        hb = flip(gb, "dp", 2, "grads_b")
        expert_inputs = [both(xa, ya), both(xb, yb)]
        expert_grads = [both(ga, ha), both(gb, hb)]
        kept, own_sums, other_sums = zip(
            *[expert_rows(r, r.shape[0] // 2, g) for r, g in zip(expert_inputs, expert_grads)]
        )

        s_z2 = flip(other_sums[0][2 * c :], "dp", 2, "sums_z2")
        r_z2 = total(own_sums[0][2 * c :], s_z2)
        s_z3 = flip(other_sums[1][2 * c :], "dp", 2, "sums_z3")
        r_z3 = total(own_sums[1][2 * c :], s_z3)
        s_near = jnp.concatenate([other_sums[0][: 2 * c], other_sums[1][: 2 * c]], axis=0)
        s_near = flip(after(s_near, s_z3, s_z2), "dp", 2, "sums_near")
        s_near = after(s_near, r_z2, r_z3)
        r_near = [total(own_sums[n][: 2 * c], s_near[2 * n * c : 2 * (n + 1) * c]) for n in range(2)]
        back = {0: r_near[0][:c]}
        for rows, first in ((r_z2, 4), (r_z3, 6)):
            for n in range(2):
                back[first + n] = flip(rows[n * c : (n + 1) * c], "expert", first + n, f"R{first + n}")
        own, other = grad_halves(expert_inputs, expert_grads, after(kept, other_sums[1]))
        other = flip(after(other, back[4], back[5], s_near), "dp", 1, "weight_grads")
        for rows, k in ((r_near[0][c:], 1), (r_near[1][:c], 2), (r_near[1][c:], 3)):
            back[k] = flip(after(rows, back[4], back[5]), "expert", k, f"returned_{k}")
        grads = grad_totals(own, other)
        grad_inputs = sum(
            by_rows(after(pick(filled, ks), needed), jnp.concatenate([back[k] for k in ks], axis=0))
            for ks, needed in (((0, 1, 4, 5), ()), ((2, 3, 6, 7), grads))
        ).astype(BF16)
    else:
        weighted = slot_weights(filled, routes, route_weights, experts)

        def exchange(rows):
            got = lax.all_to_all(
                rows.reshape(expert_count, capacity, features), "expert", split_axis=0, concat_axis=0, tiled=True
            )
            return got.reshape(-1, features)

        gate_weight, up_weight, down_weight = join_weights(*(flip(w[0], "dp", 1) for w in (w_gate, w_up, w_down)))
        beside = flip(jnp.concatenate([teacher, across], axis=0), "dp", 1)
        partner_teacher = partner_rows(teacher, across, beside, partner)
        aligned = jnp.dot(alignment, partner_teacher, preferred_element_type=F32)
        cotangent = (layer_out.astype(F32) - aligned).astype(BF16)
        x_rows = exchange(spread(filled.reshape(-1, tok_rows), inputs))
        g_rows = exchange(spread(weighted.reshape(-1, tok_rows), cotangent))
        expert_inputs = [both(x_rows, flip(x_rows, "dp", 2))]
        expert_grads = [both(g_rows, flip(g_rows, "dp", 2))]
        one, own, other = expert_rows(expert_inputs[0], x_rows.shape[0], expert_grads[0])
        kept = [one]
        back = exchange(total(own, flip(other, "dp", 2)))
        grad_inputs = by_rows(filled.reshape(-1, tok_rows), back).astype(BF16)
        own, other = grad_halves(expert_inputs, expert_grads, kept)
        grads = grad_totals(own, flip(other, "dp", 1))
    return grad_inputs, *grads


def solution(mesh):
    tokens = P(("expert", "dp"), None)
    columns, rows = P("expert", None, "dp"), P("expert", "dp", None)
    return jax.shard_map(
        per_device,
        mesh=mesh,
        in_specs=(tokens,) * 6 + (P(("expert", "dp")), columns, columns, rows),
        out_specs=(tokens, columns, columns, rows),
        check_vma=False,
    )
```
